32 devices in a mesh: ctx: 8 (over y, x, core), head: 4 (over z).
Axes of the slice: x: 2, y: 2, z: 4, core: 2. Of those that a mesh axis runs over, the one named last changes fastest.
Arguments:
- x_in: bfloat16 [12288, 8192], P(('ctx', 'head')), may hold values from -6 to 6
- dt_raw: bfloat16 [12288, 128], P(('ctx', 'head')), may hold values from -3 to 3
- bc_in: bfloat16 [12288, 256], P(('ctx', 'head')), may hold values from -6 to 6
- z_in: bfloat16 [12288, 8192], P(('ctx', 'head')), may hold values from -6 to 6
- conv_x: float32 [4, 8192], P(None, 'head'), may hold values from -3 to 3
- bias_x: float32 [8192], P('head'), may hold values from -3 to 3
- conv_bc: float32 [4, 256], replicated, may hold values from -3 to 3
- bias_bc: float32 [256], replicated, may hold values from -3 to 3
- dt_bias: float32 [128], P('head'), may hold values from -0.5 to 0.5
- a_log: float32 [128], P('head'), may hold values from -16 to -2
- d_skip: float32 [128], P('head'), may hold values from 0.5 to 1.5
- norm_gain: float32 [8192], replicated, may hold values from 0.5 to 1.5
Outputs:
- mixed: bfloat16 [12288, 8192], P(('ctx', 'head'))
The draws below stay inside these ranges and needn't reach their ends.
All inputs are finite; a program needn't handle non-finite values.
Results may differ from the reference program's by a relative error of at most 0.0015.
The reference program's roundings to bfloat16 on the way count: a program that leaves them out, or rounds other values in their place, can miss the bound.
Values may be sent and summed in bfloat16 or wider, within the bound.
A program may use at most 128 MiB of HBM per device.

```python
import jax
import jax.numpy as jnp
from jax import lax

NHEADS = 128
HEADDIM = 64
STATE = 128
BLOCK = 256
INNER = 8192
TOKENS = 12288


def draw_a_log(key, part):
    key_pick = jax.random.fold_in(key, 11)
    key_slow = jax.random.fold_in(key, 12)
    key_fast = jax.random.fold_in(key, 13)
    quick = jax.random.bernoulli(key_pick, 0.5, (NHEADS,))
    slow_rate = jax.random.uniform(key_slow, (NHEADS,), jnp.float32, 0.3, 1.0) / TOKENS
    fast_rate = jnp.exp(jax.random.uniform(key_fast, (NHEADS,), jnp.float32, jnp.log(1.0 / 40.0), jnp.log(1.0 / 15.0)))
    return jnp.log(jnp.where(quick, fast_rate, slow_rate)).astype(jnp.float32)


def levels(rng, extent, pieces, low, high):
    factor_of, own = 1.0, jax.random.fold_in(rng, 6)
    for dim, blocks in pieces:
        heights = jnp.exp(jax.random.uniform(jax.random.fold_in(own, dim), (blocks,), jnp.float32, low / len(pieces), high / len(pieces)))
        factor_of = factor_of * jnp.repeat(heights, extent[dim] // blocks).reshape([-1 if axis == dim else 1 for axis in range(len(extent))])
    return factor_of


def normal_values(own_key, extent, scale, most, shards=(), dtype=jnp.bfloat16):
    array = scale * jax.random.normal(own_key, extent, jnp.float32)
    if shards:
        array = array * levels(own_key, extent, shards, -0.22, 0.18)
    return jnp.clip(array, -most, most).astype(dtype)


def setup_inputs(seed: int = 0) -> dict:
    seeds = jax.random.split(jax.random.key(seed), 13)
    x_in = normal_values(seeds[0], (TOKENS, INNER), 1.0, 6.0, ((0, 32),))
    dt_raw = normal_values(seeds[1], (TOKENS, NHEADS), 0.5, 3.0, ((0, 32),))
    bc_in = normal_values(seeds[2], (TOKENS, 2 * STATE), 1.0, 6.0, ((0, 32),))
    z_in = normal_values(seeds[3], (TOKENS, INNER), 1.0, 6.0, ((0, 32),))
    conv_x = normal_values(seeds[4], (4, INNER), 0.5, 3.0, ((1, 4),), jnp.float32)
    bias_x = normal_values(seeds[5], (INNER,), 0.5, 3.0, ((0, 4),), jnp.float32)
    conv_bc = normal_values(seeds[6], (4, 2 * STATE), 0.5, 3.0, (), jnp.float32)
    bias_bc = normal_values(seeds[7], (2 * STATE,), 0.5, 3.0, (), jnp.float32)
    dt_bias = jnp.clip(jax.random.uniform(seeds[8], (NHEADS,), jnp.float32, -0.5, 0.5) * levels(seeds[8], (NHEADS,), ((0, 4),), -0.4, 0.0), -0.5, 0.5)
    a_log = draw_a_log(jax.random.fold_in(seeds[12], 71), 0)
    d_skip = jnp.clip(0.5 + 1.0 * jax.random.uniform(seeds[10], (NHEADS,), jnp.float32) ** levels(seeds[10], (NHEADS,), ((0, 4),), -0.2, 0.2), 0.5, 1.5)
    norm_gain = jnp.clip(1.0 + 0.1 * jax.random.normal(seeds[11], (INNER,), jnp.float32), 0.5, 1.5)
    return {"x_in": x_in, "dt_raw": dt_raw, "bc_in": bc_in, "z_in": z_in, "conv_x": conv_x, "bias_x": bias_x, "conv_bc": conv_bc, "bias_bc": bias_bc, "dt_bias": dt_bias, "a_log": a_log, "d_skip": d_skip, "norm_gain": norm_gain}


def causal_conv(values, taps, offset):
    widths = values.shape[1]
    padded = jnp.concatenate([jnp.zeros((3, widths), jnp.float32), values.astype(jnp.float32)], 0)
    summed = offset[None, :] + taps[0] * padded[0:-3] + taps[1] * padded[1:-2] + taps[2] * padded[2:-1] + taps[3] * padded[3:]
    return jax.nn.silu(summed).astype(jnp.bfloat16)

def reference(x_in, dt_raw, bc_in, z_in, conv_x, bias_x, conv_bc, bias_bc, dt_bias, a_log, d_skip, norm_gain):
    x_conv = causal_conv(x_in, conv_x, bias_x)
    bc_conv = causal_conv(bc_in, conv_bc, bias_bc)
    b_mat = bc_conv[:, :STATE]
    c_mat = bc_conv[:, STATE:]
    step_size = jax.nn.softplus(dt_raw.astype(jnp.float32) + dt_bias[None, :])
    log_decay = step_size * (-jnp.exp(a_log))[None, :]
    nblk = TOKENS // BLOCK
    x_blk = x_conv.reshape(nblk, BLOCK, NHEADS, HEADDIM)
    b_blk = b_mat.reshape(nblk, BLOCK, STATE)
    c_blk = c_mat.reshape(nblk, BLOCK, STATE)
    dt_blk = step_size.reshape(nblk, BLOCK, NHEADS)
    la_blk = log_decay.reshape(nblk, BLOCK, NHEADS)
    lower = jnp.arange(BLOCK)[:, None] >= jnp.arange(BLOCK)[None, :]

    def advance(h_state, inputs):
        x_now, b_now, c_now, dt_now, la_now = inputs
        cum_sum = jnp.cumsum(la_now, axis=0)
        scores = jnp.dot(c_now, b_now.T, preferred_element_type=jnp.float32)
        cum_t = cum_sum.T
        spread = jnp.exp(jnp.where(lower[None], cum_t[:, :, None] - cum_t[:, None, :], -1e+30))
        m_mat = (scores[None] * spread * dt_now.T[:, None, :]).astype(jnp.bfloat16)
        y_diag = jnp.einsum('hts,shp->thp', m_mat.astype(jnp.float32), x_now.astype(jnp.float32))
        h_bf = h_state.astype(jnp.bfloat16)
        y_off = jnp.einsum('tn,hnp->thp', c_now.astype(jnp.float32), h_bf.astype(jnp.float32)) * jnp.exp(cum_sum)[:, :, None]
        y_out = (y_diag + y_off + d_skip[None, :, None] * x_now.astype(jnp.float32)).astype(jnp.bfloat16)
        weight = jnp.exp(cum_sum[-1][None, :] - cum_sum) * dt_now
        b_weighted = (b_now.astype(jnp.float32)[:, None, :] * weight[:, :, None]).astype(jnp.bfloat16)
        st_new = jnp.einsum('qhn,qhp->hnp', b_weighted.astype(jnp.float32), x_now.astype(jnp.float32))
        h_next = h_state * jnp.exp(cum_sum[-1])[:, None, None] + st_new
        return (h_next, y_out)
    start = jnp.zeros((NHEADS, STATE, HEADDIM), jnp.float32)
    _, y_all = lax.scan(advance, start, (x_blk, b_blk, c_blk, dt_blk, la_blk))
    y_flat = y_all.reshape(TOKENS, INNER)
    gated = y_flat.astype(jnp.float32) * jax.nn.silu(z_in.astype(jnp.float32))
    mean_sq = lax.optimization_barrier(jnp.mean(gated * gated, axis=-1, keepdims=True))
    return (gated * lax.rsqrt(mean_sq + 1e-05) * norm_gain[None, :]).astype(jnp.bfloat16)
```

```python
import functools

import jax
import jax.numpy as jnp
from jax import lax
from jax.experimental import pallas as pl
from jax.experimental.pallas import tpu as pltpu
from jax.sharding import PartitionSpec as P

BLOCK = 256


def from_behind(value, axis, by):
    count = lax.axis_size(axis)
    pairs = [(i, i + by) for i in range(count) if 0 <= i + by < count]
    return lax.ppermute(value, axis, pairs)


def entering(value, axis, combine, identity):
    count, place = (lax.axis_size(axis), lax.axis_index(axis))
    everything = jax.tree.map(lambda part: lax.all_gather(part, axis), value)
    start = jax.tree.map(
        lambda part, zero: jnp.broadcast_to(jnp.asarray(zero, part.dtype), part.shape),
        value,
        identity,
    )

    def step(k, before):
        reached = k < place
        new = combine(before, jax.tree.map(lambda part: part[k], everything))
        return jax.tree.map(lambda a, b: jnp.where(reached, a, b), new, before)

    return lax.fori_loop(0, count, step, start)


def causal_conv(values, rim_rows, taps, offset):
    padded = jnp.concatenate([rim_rows.astype(jnp.float32), values.astype(jnp.float32)], 0)
    summed = (
        offset[None, :]
        + taps[0] * padded[0:-3]
        + taps[1] * padded[1:-2]
        + taps[2] * padded[2:-1]
        + taps[3] * padded[3:]
    )
    return jax.nn.silu(summed).astype(jnp.bfloat16)


def per_device_by_heads(
    x_in, dt_raw, bc_in, z_in, conv_x, bias_x, conv_bc, bias_bc, dt_bias, a_log, d_skip, norm_gain
):
    x_group, dt_group = (
        lax.all_to_all(x_in, "head", split_axis=1, concat_axis=0, tiled=True),
        lax.all_to_all(dt_raw, "head", split_axis=1, concat_axis=0, tiled=True),
    )
    bc_group = lax.all_gather(bc_in, "head", axis=0, tiled=True)
    tail_rows = jnp.concatenate([x_group[-3:], bc_group[-3:]], 1)
    rim_rows = from_behind(tail_rows, "ctx", 1)
    x_width = x_group.shape[1]
    x_conv = causal_conv(x_group, rim_rows[:, :x_width], conv_x, bias_x)
    bc_conv = causal_conv(bc_group, rim_rows[:, x_width:], conv_bc, bias_bc)
    state_size = bc_in.shape[1] // 2
    seg_rows = x_group.shape[0]
    head_count = dt_group.shape[1]
    head_width = x_width // head_count
    nblk = seg_rows // BLOCK
    x_blk = x_conv.reshape(nblk, BLOCK, head_count, head_width)
    b_blk = bc_conv[:, :state_size].reshape(nblk, BLOCK, state_size)
    c_blk = bc_conv[:, state_size:].reshape(nblk, BLOCK, state_size)
    step_size = jax.nn.softplus(dt_group.astype(jnp.float32) + dt_bias[None, :])
    log_decay = step_size * (-jnp.exp(a_log))[None, :]
    dt_blk = step_size.reshape(nblk, BLOCK, head_count)
    cum_sum = jnp.cumsum(log_decay.reshape(nblk, BLOCK, head_count), axis=1)
    scores = jnp.einsum("ctn,csn->cts", c_blk, b_blk, preferred_element_type=jnp.float32)
    cum_t = cum_sum.transpose(0, 2, 1)
    lower = jnp.arange(BLOCK)[:, None] >= jnp.arange(BLOCK)[None, :]
    spread = jnp.exp(
        jnp.where(lower[None, None], cum_t[:, :, :, None] - cum_t[:, :, None, :], -1e30)
    )
    m_mat = (scores[:, None] * spread * dt_blk.transpose(0, 2, 1)[:, :, None, :]).astype(
        jnp.bfloat16
    )
    y_diag = jnp.einsum("chts,cshp->cthp", m_mat, x_blk, preferred_element_type=jnp.float32)
    weight = jnp.exp(cum_sum[:, -1:, :] - cum_sum) * dt_blk
    b_weighted = (b_blk.astype(jnp.float32)[:, :, None, :] * weight[:, :, :, None]).astype(
        jnp.bfloat16
    )
    st_new = jnp.einsum("cqhn,cqhp->chnp", b_weighted, x_blk, preferred_element_type=jnp.float32)
    totals = cum_sum[:, -1, :]
    local_states = [jnp.zeros((head_count, state_size, head_width), jnp.float32)]
    for blk_i in range(nblk):
        local_states.append(
            local_states[-1] * jnp.exp(totals[blk_i])[:, None, None] + st_new[blk_i]
        )
    summary = local_states[nblk]
    seg_decay = jnp.sum(totals, axis=0)

    def combine_pair(earlier, later):
        return (earlier[0] + later[0], earlier[1] * jnp.exp(later[0])[:, None, None] + later[1])

    identity = (jnp.zeros_like(seg_decay), jnp.zeros_like(summary))
    _, incoming = entering((seg_decay, summary), "ctx", combine_pair, identity)
    prior = jnp.cumsum(totals, axis=0) - totals
    h_in = incoming[None] * jnp.exp(prior)[:, :, None, None] + jnp.stack(local_states[:nblk], 0)
    h_bf = h_in.astype(jnp.bfloat16)
    y_off = (
        jnp.einsum("ctn,chnp->cthp", c_blk, h_bf, preferred_element_type=jnp.float32)
        * jnp.exp(cum_sum)[:, :, :, None]
    )
    y_out = (y_diag + y_off + d_skip[None, None, :, None] * x_blk.astype(jnp.float32)).astype(
        jnp.bfloat16
    )
    y_tokens = lax.all_to_all(
        y_out.reshape(seg_rows, x_width), "head", split_axis=0, concat_axis=1, tiled=True
    )
    gated = y_tokens.astype(jnp.float32) * jax.nn.silu(z_in.astype(jnp.float32))
    mean_sq = jnp.mean(gated * gated, axis=-1, keepdims=True)
    return (gated * lax.rsqrt(mean_sq + 1e-05) * norm_gain[None, :]).astype(jnp.bfloat16)


HALF = 128
RIM = 16
STEP_HEADS = 8
VMEM_BYTES = 56 * 1024 * 1024


def silu(u):
    return u / (1.0 + jnp.exp(-u))


def rows_conv(halo, values, taps, offset):
    rows, at = values.shape[0], halo.shape[0] - 3
    padded = jnp.concatenate([halo.astype(jnp.float32), values.astype(jnp.float32)], 0)
    summed = (
        offset
        + taps[0:1] * padded[at : at + rows]
        + taps[1:2] * padded[at + 1 : at + 1 + rows]
        + taps[2:3] * padded[at + 2 : at + 2 + rows]
        + taps[3:4] * padded[at + 3 : at + 3 + rows]
    )
    return silu(summed).astype(jnp.bfloat16)


def prep_kernel(
    odd_ref, bc_ref, halo_ref, ebc_ref, taps_ref, bias_ref, dt_ref, edt_ref, dtb_ref, alog_ref,
    c_ref, bt_ref, s_ref, g_ref, gt_ref, dtt_ref, wt_ref, ecs_ref, log_ref,
):
    odd = odd_ref[0] == 1
    taps, bias = taps_ref[...], bias_ref[...]
    ebc = ebc_ref[...].astype(jnp.float32)
    bcc = jnp.concatenate(
        [
            rows_conv(ebc[:RIM], ebc[RIM:], taps, bias).astype(jnp.float32),
            rows_conv(halo_ref[...], bc_ref[...], taps, bias).astype(jnp.float32),
        ],
        0,
    ).astype(jnp.bfloat16)
    n = bcc.shape[1] // 2
    b, c = bcc[:, :n], bcc[:, n:]
    c_ref[...] = c[HALF:]
    bt_ref[...] = b.astype(jnp.float32).T.astype(jnp.bfloat16)

    def score(i, j):
        return lax.dot_general(
            c[i * HALF : (i + 1) * HALF],
            b[j * HALF : (j + 1) * HALF],
            (((1,), (1,)), ((), ())),
            preferred_element_type=jnp.float32,
        )

    for i in range(3):
        s_ref[i] = score(i + 1, i + 1)
    s_ref[3] = jnp.where(odd, score(3, 2), score(2, 1))
    s_ref[4] = score(1, 0)

    raw = [edt_ref[...].astype(jnp.float32)[RIM:], dt_ref[...].astype(jnp.float32)]
    u = jnp.concatenate(raw, 0) + dtb_ref[...]
    row = lax.broadcasted_iota(jnp.int32, u.shape, 0)
    dt = jnp.maximum(u, 0.0) + jnp.log1p(jnp.exp(-jnp.abs(u)))
    dt = jnp.where(jnp.logical_and(row < HALF, jnp.logical_not(odd)), 0.0, dt)
    la = dt * (-jnp.exp(alog_ref[...]))
    rows = la.shape[0]
    at = lax.broadcasted_iota(jnp.int32, (rows, rows), 0)
    of = lax.broadcasted_iota(jnp.int32, (rows, rows), 1)
    g = jnp.dot(
        (at >= of).astype(jnp.float32), la,
        precision=lax.Precision.HIGHEST, preferred_element_type=jnp.float32,
    )
    cut = jnp.where(odd, 2 * HALF, 3 * HALF)
    g_cut = jnp.where(odd, g[2 * HALF - 1 : 2 * HALF], g[3 * HALF - 1 : 3 * HALF])
    g_end = g[rows - 1 : rows]
    first = row < cut
    ecs_ref[...] = jnp.exp(g - jnp.where(first, 0.0, g_cut))[HALF:]
    weight = jnp.exp(jnp.where(first, g_cut, g_end) - g) * dt
    g_ref[...] = g[HALF:]
    gt_ref[...] = g.T
    dtt_ref[...] = dt.T
    wt_ref[...] = weight.T
    log_ref[...] = jnp.concatenate(
        [g_cut, g_end - g_cut, jnp.where(odd, g_end, g_cut), jnp.zeros((5, g.shape[1]))], 0
    )


def states_kernel(
    odd_ref, x_ref, halo_ref, ex_ref, par_ref, bt_ref, wt_ref, dec_ref, xc_ref, st_ref, sum_ref
):
    odd = odd_ref[0] == 1
    par = par_ref[...]
    ex = ex_ref[...].astype(jnp.float32)
    xc_ref[:HALF] = rows_conv(ex[:RIM], ex[RIM:], par[0:4], par[4:5])
    xc_ref[HALF:] = rows_conv(halo_ref[...], x_ref[...], par[0:4], par[4:5])
    bt = bt_ref[...].astype(jnp.float32)
    wt = wt_ref[...]
    n = bt.shape[0]
    left = lax.broadcasted_iota(jnp.int32, (n, 128), 1) < 64
    for pair in range(STEP_HEADS // 2):
        lanes = slice(pair * 128, pair * 128 + 128)
        parts = []
        for i in range(4):
            cols = slice(i * HALF, (i + 1) * HALF)
            both = jnp.concatenate(
                [
                    (bt[:, cols] * wt[2 * pair + k : 2 * pair + k + 1, cols]).astype(jnp.bfloat16)
                    for k in range(2)
                ],
                0,
            )
            full = jnp.dot(both, xc_ref[cols, lanes], preferred_element_type=jnp.float32)
            parts.append(jnp.where(left, full[:n], full[n:]))
        st_first = parts[1] + jnp.where(odd, parts[0], parts[2])
        both_blocks = st_first * dec_ref[1:2, lanes] + (parts[2] + parts[3])
        st_ref[0, :, lanes] = st_first
        sum_ref[0, :, lanes] = jnp.where(odd, both_blocks, st_first)


def diag_kernel(odd_ref, xc_ref, s_ref, g_ref, gt_ref, dtt_ref, par_ref, y_ref):
    shift = odd_ref[0]
    odd = shift == 1
    g, gt, dtt = g_ref[0], gt_ref[...], dtt_ref[...]
    t_at = lax.broadcasted_iota(jnp.int32, (HALF, HALF), 0)
    s_at = lax.broadcasted_iota(jnp.int32, (HALF, HALF), 1)
    lower = t_at >= s_at
    left = s_at < 64
    subs = [slice(i * HALF, (i + 1) * HALF) for i in range(3)]
    g_off = jnp.where(odd, g[subs[2]], g[subs[1]])
    behind = [slice(i * HALF, (i + 1) * HALF) for i in range(4)]
    gt_off = jnp.where(odd, gt[:, behind[2]], gt[:, behind[1]])
    dtt_off = jnp.where(odd, dtt[:, behind[2]], dtt[:, behind[1]])
    x_off = xc_ref[pl.ds(pl.multiple_of(HALF + shift * HALF, HALF), HALF), :]
    tiles = [(g[subs[i]], gt[:, at], dtt[:, at], xc_ref[at, :]) for i, at in enumerate(behind[1:])]
    tiles.append((g_off, gt_off, dtt_off, x_off))
    tiles.append((g[subs[0]], gt[:, behind[0]], dtt[:, behind[0]], xc_ref[behind[0], :]))
    for pair in range(STEP_HEADS // 2):
        lanes = slice(pair * 128, pair * 128 + 128)
        results = []
        for i, (g_t, g_s, dt_s, x_s) in enumerate(tiles):
            both = []
            for k in range(2):
                h = 2 * pair + k
                gap = g_t[:, h : h + 1] - g_s[h : h + 1]
                if i < 3:
                    gap = jnp.where(lower, gap, -1e30)
                both.append(
                    (s_ref[i] * jnp.exp(gap) * dt_s[h : h + 1]).astype(jnp.bfloat16)
                )
            full = jnp.dot(
                jnp.concatenate(both, 0), x_s[:, lanes], preferred_element_type=jnp.float32
            )
            results.append(jnp.where(left, full[:HALF], full[HALF:]))
        skip = par_ref[5:6, lanes]
        for i in range(3):
            y = results[i] + skip * tiles[i][3][:, lanes].astype(jnp.float32)
            if i == 0:
                y = y + results[4]
            if i == 1:
                y = y + jnp.where(odd, 0.0, results[3])
            if i == 2:
                y = y + jnp.where(odd, results[3], 0.0)
            y_ref[subs[i], lanes] = y


def gate_kernel(
    odd_ref, y_ref, c_ref, ecs_ref, h_ref, st_ref, dec_ref, z_ref, gain_ref, out_ref, held
):
    early = pl.program_id(0) < 2 - odd_ref[0]
    c = c_ref[...]
    ecs = ecs_ref[...]
    left = lax.broadcasted_iota(jnp.int32, (HALF, 128), 1) < 64
    groups, _, width = h_ref.shape
    wide = STEP_HEADS * 64
    square = jnp.zeros((HALF, 128), jnp.float32)
    for start in range(0, groups * width, wide):
        group, off = divmod(start, width)
        cols = slice(off, off + wide)
        h = h_ref[group, :, cols]
        later = h * dec_ref[0:1, start : start + wide] + st_ref[group, :, cols]
        hb = jnp.where(early, h, later).astype(jnp.bfloat16)
        far = jnp.dot(c, hb, preferred_element_type=jnp.float32)
        for pair in range(STEP_HEADS // 2):
            head = start // 64 + 2 * pair
            lanes = slice(start + pair * 128, start + pair * 128 + 128)
            scale = jnp.where(left, ecs[:, head : head + 1], ecs[:, head + 1 : head + 2])
            y = y_ref[:, lanes] + far[:, pair * 128 : pair * 128 + 128] * scale
            y = y.astype(jnp.bfloat16).astype(jnp.float32)
            gated = y * silu(z_ref[:, lanes].astype(jnp.float32))
            held[:, lanes] = gated
            square = square + gated * gated
    mean = jnp.sum(square, axis=1, keepdims=True) / (groups * width)
    scale = lax.rsqrt(mean + 1e-5)
    for start in range(0, groups * width, wide):
        lanes = slice(start, start + wide)
        out_ref[:, lanes] = (held[:, lanes] * scale * gain_ref[:, lanes]).astype(jnp.bfloat16)


def params(**more):
    return pltpu.CompilerParams(vmem_limit_bytes=VMEM_BYTES, **more)


def per_device(
    x_in, dt_raw, bc_in, z_in, conv_x, bias_x, conv_bc, bias_bc, dt_bias, a_log, d_skip, norm_gain
):
    f32, bf16 = jnp.float32, jnp.bfloat16
    n_ctx, n_head = lax.axis_size("ctx"), lax.axis_size("head")
    ctx, zed = lax.axis_index("ctx"), lax.axis_index("head")
    rows, width = x_in.shape
    heads = dt_raw.shape[1]
    state = bc_in.shape[1] // 2
    group_width = width // n_head
    group_heads = heads // n_head
    odd = (zed % 2).astype(jnp.int32).reshape(1)

    small = jnp.concatenate([dt_bias, a_log, d_skip])
    small = jnp.pad(small, (0, group_width - small.shape[0]))
    mine = jnp.concatenate([conv_x, bias_x[None], small[None]], 0)
    table = lax.all_gather(mine, "head")
    par = jnp.concatenate([table[g] for g in range(n_head)], 1)
    vectors = table[:, 5, : 3 * group_heads].reshape(n_head, 3, group_heads)
    vectors = vectors.transpose(1, 0, 2).reshape(3, heads)
    skip = jnp.repeat(vectors[2], width // heads)
    par = jnp.concatenate([par[:5], skip[None], jnp.zeros((2, width), f32)], 0)
    count = n_ctx * n_head
    rim = jnp.concatenate([x_in[-RIM:], bc_in[-RIM:]], 1)
    rim = lax.ppermute(rim, ("ctx", "head"), [(i, i + 1) for i in range(count - 1)])
    halo_x, halo_bc = rim[:, :width], rim[:, width:]
    last = rows - HALF - RIM
    to_odd = [(i, i + 1) for i in range(0, n_head, 2)]
    extra_x = lax.ppermute(x_in[last:], "head", to_odd)
    extra_small = lax.ppermute(jnp.concatenate([bc_in[last:], dt_raw[last:]], 1), "head", to_odd)
    extra_bc, extra_dt = extra_small[:, : 2 * state], extra_small[:, 2 * state :]
    deep = rows + HALF

    smem = pl.BlockSpec(memory_space=pltpu.SMEM)
    vmem = pl.BlockSpec(memory_space=pltpu.VMEM)
    shape = jax.ShapeDtypeStruct
    c, bt, scores, g, gt, dtt, wt, ecs, logs = pl.pallas_call(
        prep_kernel,
        in_specs=[smem] + [vmem] * 9,
        out_specs=[vmem] * 9,
        out_shape=[
            shape((rows, state), bf16),
            shape((state, deep), bf16),
            shape((5, HALF, HALF), f32),
            shape((rows, heads), f32),
            shape((heads, deep), f32),
            shape((heads, deep), f32),
            shape((heads, deep), f32),
            shape((rows, heads), f32),
            shape((8, heads), f32),
        ],
        compiler_params=params(),
        name="prep",
    )(
        odd, bc_in, halo_bc, extra_bc, conv_bc, bias_bc[None], dt_raw, extra_dt,
        vectors[0:1], vectors[1:2],
    )
    decays = jnp.repeat(jnp.exp(logs), width // heads, axis=1)
    all_logs = lax.all_gather(logs[2], ("ctx", "head")).reshape(n_ctx, n_head, heads)

    steps = heads // STEP_HEADS
    wide = STEP_HEADS * (width // heads)
    per_group = group_width // wide
    tall = pl.BlockSpec((rows, wide), lambda i: (0, i))
    tall_deep = pl.BlockSpec((deep, wide), lambda i: (0, i))
    eight = pl.BlockSpec((8, wide), lambda i: (0, i))
    by_group = pl.BlockSpec((1, state, wide), lambda i: (i // per_group, 0, i % per_group))
    row_heads = pl.BlockSpec((STEP_HEADS, deep), lambda i: (i, 0))

    def whole(*dims):
        return pl.BlockSpec(dims, lambda i: (0,) * len(dims))

    grouped = shape((n_head, state, group_width), f32)
    xc, st_first, summary = pl.pallas_call(
        states_kernel,
        grid=(steps,),
        in_specs=[
            smem,
            tall,
            pl.BlockSpec((RIM, wide), lambda i: (0, i)),
            pl.BlockSpec((RIM + HALF, wide), lambda i: (0, i)),
            eight,
            whole(state, deep),
            row_heads,
            eight,
        ],
        out_specs=[tall_deep, by_group, by_group],
        out_shape=[shape((deep, width), bf16), grouped, grouped],
        compiler_params=params(),
        cost_estimate=pl.CostEstimate(
            flops=2 * rows * state * width, bytes_accessed=20 * 2**20, transcendentals=rows * width
        ),
        name="states",
    )(odd, x_in, halo_x, extra_x, par, bt, wt, decays)

    parts = lax.all_to_all(summary, "head", split_axis=0, concat_axis=0, tiled=True)

    g_steps = g.reshape(rows, steps, STEP_HEADS).transpose(1, 0, 2)
    y_near = pl.pallas_call(
        diag_kernel,
        grid=(steps,),
        in_specs=[
            smem,
            tall_deep,
            whole(5, HALF, HALF),
            pl.BlockSpec((1, rows, STEP_HEADS), lambda i: (i, 0, 0)),
            row_heads,
            row_heads,
            eight,
        ],
        out_specs=tall,
        out_shape=shape((rows, width), f32),
        compiler_params=params(),
        cost_estimate=pl.CostEstimate(
            flops=10 * 2 * HALF * HALF * width,
            bytes_accessed=20 * 2**20,
            transcendentals=5 * HALF * HALF * heads,
        ),
        name="diag",
    )(odd, xc, scores, g_steps, gt, dtt, par)

    own_logs = lax.dynamic_slice_in_dim(all_logs, zed * group_heads, group_heads, 2)

    def lanes_of(log):
        return jnp.repeat(jnp.exp(log), width // heads)[None, :]

    total = parts[0]
    for k in range(1, n_head):
        total = total * lanes_of(own_logs[ctx, k]) + parts[k]
    seg_logs = own_logs.sum(1)
    before = jnp.zeros_like(total)
    span = 1
    while span < n_ctx:
        other = lax.ppermute(total, "ctx", [(i, i ^ span) for i in range(n_ctx)])
        block_logs = seg_logs.reshape(n_ctx // span, span, group_heads).sum(1)
        block = ctx // span
        upper = block % 2 == 1
        own_dec = lanes_of(block_logs[block])
        other_dec = lanes_of(block_logs[block ^ 1])
        place = jnp.arange(n_ctx)
        inside = (place >= block * span) & (place < ctx)
        lead = lanes_of(jnp.sum(jnp.where(inside[:, None], seg_logs, 0.0), 0))
        before = jnp.where(upper, other * lead + before, before)
        total = jnp.where(upper, other * own_dec + total, total * other_dec + other)
        span *= 2
    entries = [before]
    for k in range(n_head - 1):
        entries.append(entries[-1] * lanes_of(own_logs[ctx, k]) + parts[k])
    h_in = lax.all_to_all(jnp.stack(entries), "head", split_axis=0, concat_axis=0, tiled=True)

    tile = pl.BlockSpec((HALF, width), lambda i: (i, 0))
    narrow = pl.BlockSpec((HALF, heads), lambda i: (i, 0))
    return pl.pallas_call(
        gate_kernel,
        grid=(rows // HALF,),
        in_specs=[
            smem,
            tile,
            pl.BlockSpec((HALF, state), lambda i: (i, 0)),
            narrow,
            whole(n_head, state, group_width),
            whole(n_head, state, group_width),
            whole(8, width),
            tile,
            whole(1, width),
        ],
        out_specs=tile,
        out_shape=shape((rows, width), bf16),
        scratch_shapes=[pltpu.VMEM((HALF, width), f32)],
        compiler_params=params(),
        name="gate",
    )(odd, y_near, c, ecs, h_in, st_first, decays, z_in, norm_gain[None])


def solution(mesh):
    in_specs = (
        P(("ctx", "head"), None),
        P(("ctx", "head"), None),
        P(("ctx", "head"), None),
        P(("ctx", "head"), None),
        P(None, "head"),
        P("head"),
        P(),
        P(),
        P("head"),
        P("head"),
        P("head"),
        P(),
    )
    out_specs = P(("ctx", "head"), None)

    def run(x_in, *rest):
        n_ctx, n_head = mesh.shape["ctx"], mesh.shape["head"]
        rows = x_in.shape[0] // (n_ctx * n_head)
        fits = 2 * rows == 3 * BLOCK and n_head % 2 == 0 and n_ctx & (n_ctx - 1) == 0
        body = per_device if fits else per_device_by_heads
        return jax.shard_map(
            body, mesh=mesh, in_specs=in_specs, out_specs=out_specs, check_vma=False
        )(x_in, *rest)

    return run
```

```python
import functools

import jax
import jax.numpy as jnp
from jax import lax
from jax.experimental import pallas as pl
from jax.experimental.pallas import tpu as pltpu
from jax.sharding import PartitionSpec as P

BLOCK = 256


def from_behind(value, axis, by):
    count = lax.axis_size(axis)
    pairs = [(i, i + by) for i in range(count) if 0 <= i + by < count]
    return lax.ppermute(value, axis, pairs)


def entering(value, axis, combine, identity):
    count, place = (lax.axis_size(axis), lax.axis_index(axis))
    everything = jax.tree.map(lambda part: lax.all_gather(part, axis), value)
    start = jax.tree.map(
        lambda part, zero: jnp.broadcast_to(jnp.asarray(zero, part.dtype), part.shape),
        value,
        identity,
    )

    def step(k, before):
        reached = k < place
        new = combine(before, jax.tree.map(lambda part: part[k], everything))
        return jax.tree.map(lambda a, b: jnp.where(reached, a, b), new, before)

    return lax.fori_loop(0, count, step, start)


def causal_conv(values, rim_rows, taps, offset):
    padded = jnp.concatenate([rim_rows.astype(jnp.float32), values.astype(jnp.float32)], 0)
    summed = (
        offset[None, :]
        + taps[0] * padded[0:-3]
        + taps[1] * padded[1:-2]
        + taps[2] * padded[2:-1]
        + taps[3] * padded[3:]
    )
    return jax.nn.silu(summed).astype(jnp.bfloat16)


def per_device_by_heads(
    x_in, dt_raw, bc_in, z_in, conv_x, bias_x, conv_bc, bias_bc, dt_bias, a_log, d_skip, norm_gain
):
    x_group, dt_group = (
        lax.all_to_all(x_in, "head", split_axis=1, concat_axis=0, tiled=True),
        lax.all_to_all(dt_raw, "head", split_axis=1, concat_axis=0, tiled=True),
    )
    bc_group = lax.all_gather(bc_in, "head", axis=0, tiled=True)
    tail_rows = jnp.concatenate([x_group[-3:], bc_group[-3:]], 1)
    rim_rows = from_behind(tail_rows, "ctx", 1)
    x_width = x_group.shape[1]
    x_conv = causal_conv(x_group, rim_rows[:, :x_width], conv_x, bias_x)
    bc_conv = causal_conv(bc_group, rim_rows[:, x_width:], conv_bc, bias_bc)
    state_size = bc_in.shape[1] // 2
    seg_rows = x_group.shape[0]
    head_count = dt_group.shape[1]
    head_width = x_width // head_count
    nblk = seg_rows // BLOCK
    x_blk = x_conv.reshape(nblk, BLOCK, head_count, head_width)
    b_blk = bc_conv[:, :state_size].reshape(nblk, BLOCK, state_size)
    c_blk = bc_conv[:, state_size:].reshape(nblk, BLOCK, state_size)
    step_size = jax.nn.softplus(dt_group.astype(jnp.float32) + dt_bias[None, :])
    log_decay = step_size * (-jnp.exp(a_log))[None, :]
    dt_blk = step_size.reshape(nblk, BLOCK, head_count)
    cum_sum = jnp.cumsum(log_decay.reshape(nblk, BLOCK, head_count), axis=1)
    scores = jnp.einsum("ctn,csn->cts", c_blk, b_blk, preferred_element_type=jnp.float32)
    cum_t = cum_sum.transpose(0, 2, 1)
    lower = jnp.arange(BLOCK)[:, None] >= jnp.arange(BLOCK)[None, :]
    spread = jnp.exp(
        jnp.where(lower[None, None], cum_t[:, :, :, None] - cum_t[:, :, None, :], -1e30)
    )
    m_mat = (scores[:, None] * spread * dt_blk.transpose(0, 2, 1)[:, :, None, :]).astype(
        jnp.bfloat16
    )
    y_diag = jnp.einsum("chts,cshp->cthp", m_mat, x_blk, preferred_element_type=jnp.float32)
    weight = jnp.exp(cum_sum[:, -1:, :] - cum_sum) * dt_blk
    b_weighted = (b_blk.astype(jnp.float32)[:, :, None, :] * weight[:, :, :, None]).astype(
        jnp.bfloat16
    )
    st_new = jnp.einsum("cqhn,cqhp->chnp", b_weighted, x_blk, preferred_element_type=jnp.float32)
    totals = cum_sum[:, -1, :]
    local_states = [jnp.zeros((head_count, state_size, head_width), jnp.float32)]
    for blk_i in range(nblk):
        local_states.append(
            local_states[-1] * jnp.exp(totals[blk_i])[:, None, None] + st_new[blk_i]
        )
    summary = local_states[nblk]
    seg_decay = jnp.sum(totals, axis=0)

    def combine_pair(earlier, later):
        return (earlier[0] + later[0], earlier[1] * jnp.exp(later[0])[:, None, None] + later[1])

    identity = (jnp.zeros_like(seg_decay), jnp.zeros_like(summary))
    _, incoming = entering((seg_decay, summary), "ctx", combine_pair, identity)
    prior = jnp.cumsum(totals, axis=0) - totals
    h_in = incoming[None] * jnp.exp(prior)[:, :, None, None] + jnp.stack(local_states[:nblk], 0)
    h_bf = h_in.astype(jnp.bfloat16)
    y_off = (
        jnp.einsum("ctn,chnp->cthp", c_blk, h_bf, preferred_element_type=jnp.float32)
        * jnp.exp(cum_sum)[:, :, :, None]
    )
    y_out = (y_diag + y_off + d_skip[None, None, :, None] * x_blk.astype(jnp.float32)).astype(
        jnp.bfloat16
    )
    y_tokens = lax.all_to_all(
        y_out.reshape(seg_rows, x_width), "head", split_axis=0, concat_axis=1, tiled=True
    )
    gated = y_tokens.astype(jnp.float32) * jax.nn.silu(z_in.astype(jnp.float32))
    mean_sq = jnp.mean(gated * gated, axis=-1, keepdims=True)
    return (gated * lax.rsqrt(mean_sq + 1e-05) * norm_gain[None, :]).astype(jnp.bfloat16)


HALF = 128
RIM = 16
STEP_HEADS = 8
VMEM_BYTES = 56 * 1024 * 1024


def silu(u):
    return u / (1.0 + jnp.exp(-u))


def rows_conv(halo, values, taps, offset):
    rows, at = values.shape[0], halo.shape[0] - 3
    padded = jnp.concatenate([halo.astype(jnp.float32), values.astype(jnp.float32)], 0)
    summed = (
        offset
        + taps[0:1] * padded[at : at + rows]
        + taps[1:2] * padded[at + 1 : at + 1 + rows]
        + taps[2:3] * padded[at + 2 : at + 2 + rows]
        + taps[3:4] * padded[at + 3 : at + 3 + rows]
    )
    return silu(summed).astype(jnp.bfloat16)


def prep_kernel(
    odd_ref, bc_ref, halo_ref, ebc_ref, taps_ref, bias_ref, dt_ref, edt_ref, dtb_ref, alog_ref,
    c_ref, bt_ref, s_ref, g_ref, gt_ref, dtt_ref, wt_ref, ecs_ref, log_ref,
):
    odd = odd_ref[0] == 1
    taps, bias = taps_ref[...], bias_ref[...]
    ebc = ebc_ref[...].astype(jnp.float32)
    bcc = jnp.concatenate(
        [
            rows_conv(ebc[:RIM], ebc[RIM:], taps, bias).astype(jnp.float32),
            rows_conv(halo_ref[...], bc_ref[...], taps, bias).astype(jnp.float32),
        ],
        0,
    ).astype(jnp.bfloat16)
    n = bcc.shape[1] // 2
    b, c = bcc[:, :n], bcc[:, n:]
    c_ref[...] = c[HALF:]
    bt_ref[...] = b.astype(jnp.float32).T.astype(jnp.bfloat16)

    def score(i, j):
        return lax.dot_general(
            c[i * HALF : (i + 1) * HALF],
            b[j * HALF : (j + 1) * HALF],
            (((1,), (1,)), ((), ())),
            preferred_element_type=jnp.float32,
        )

    for i in range(3):
        s_ref[i] = score(i + 1, i + 1)
    s_ref[3] = jnp.where(odd, score(3, 2), score(2, 1))
    s_ref[4] = score(1, 0)

    raw = [edt_ref[...].astype(jnp.float32)[RIM:], dt_ref[...].astype(jnp.float32)]
    u = jnp.concatenate(raw, 0) + dtb_ref[...]
    row = lax.broadcasted_iota(jnp.int32, u.shape, 0)
    dt = jnp.maximum(u, 0.0) + jnp.log1p(jnp.exp(-jnp.abs(u)))
    dt = jnp.where(jnp.logical_and(row < HALF, jnp.logical_not(odd)), 0.0, dt)
    la = dt * (-jnp.exp(alog_ref[...]))
    rows = la.shape[0]
    at = lax.broadcasted_iota(jnp.int32, (rows, rows), 0)
    of = lax.broadcasted_iota(jnp.int32, (rows, rows), 1)
    g = jnp.dot(
        (at >= of).astype(jnp.float32), la,
        precision=lax.Precision.HIGHEST, preferred_element_type=jnp.float32,
    )
    cut = jnp.where(odd, 2 * HALF, 3 * HALF)
    g_cut = jnp.where(odd, g[2 * HALF - 1 : 2 * HALF], g[3 * HALF - 1 : 3 * HALF])
    g_end = g[rows - 1 : rows]
    first = row < cut
    ecs_ref[...] = jnp.exp(g - jnp.where(first, 0.0, g_cut))[HALF:]
    weight = jnp.exp(jnp.where(first, g_cut, g_end) - g) * dt
    g_ref[...] = g[HALF:]
    gt_ref[...] = g.T
    dtt_ref[...] = dt.T
    wt_ref[...] = weight.T
    log_ref[...] = jnp.concatenate(
        [
            jnp.exp(g_cut),
            jnp.exp(g_end - g_cut),
            jnp.where(odd, g_end, g_cut),
            jnp.zeros((5, g.shape[1])),
        ],
        0,
    )


def weighted(bt, wt, xc, pair, left):
    n = bt.shape[0]
    both = [(bt * wt[2 * pair + k : 2 * pair + k + 1]).astype(jnp.bfloat16) for k in range(2)]
    full = jnp.dot(jnp.concatenate(both, 0), xc, preferred_element_type=jnp.float32)
    return jnp.where(left, full[:n], full[n:])


def own_kernel(odd_ref, x_ref, halo_ref, par_ref, bt_ref, wt_ref, xc_ref, qa_ref, qb_ref):
    odd = odd_ref[0] == 1
    par = par_ref[...]
    xc = rows_conv(halo_ref[...], x_ref[...], par[0:4], par[4:5])
    xc_ref[...] = xc
    bt = bt_ref[...].astype(jnp.float32)
    wt = wt_ref[...]
    left = lax.broadcasted_iota(jnp.int32, (bt.shape[0], 128), 1) < 64
    for pair in range(STEP_HEADS // 2):
        lanes = slice(pair * 128, pair * 128 + 128)
        parts = []
        for i in range(3):
            at, cols = slice(i * HALF, (i + 1) * HALF), slice((i + 1) * HALF, (i + 2) * HALF)
            parts.append(weighted(bt[:, cols], wt[:, cols], xc[at, lanes], pair, left))
        qa_ref[0, 0, :, lanes] = parts[0] + jnp.where(odd, 0.0, parts[1])
        qb_ref[0, 0, :, lanes] = jnp.where(odd, parts[1] + parts[2], 0.0)


def extra_kernel(
    odd_ref, ex_ref, par_ref, bt_ref, wt_ref, dec_ref, qa_ref, qb_ref, xc_ref, st_ref, sum_ref
):
    odd = odd_ref[0] == 1
    par = par_ref[...]
    ex = ex_ref[...].astype(jnp.float32)
    xc = rows_conv(ex[:RIM], ex[RIM:], par[0:4], par[4:5])
    xc_ref[...] = xc
    bt = bt_ref[...].astype(jnp.float32)[:, :HALF]
    wt = wt_ref[...][:, :HALF]
    n = bt.shape[0]
    left = lax.broadcasted_iota(jnp.int32, (n, 128), 1) < 64
    for pair in range(STEP_HEADS // 2):
        lanes = slice(pair * 128, pair * 128 + 128)
        st_first = qa_ref[0, 0, :, lanes] + weighted(bt, wt, xc[:, lanes], pair, left)
        both_blocks = st_first * dec_ref[1:2, lanes] + qb_ref[0, 0, :, lanes]
        st_ref[0, 0, :, lanes] = st_first
        sum_ref[0, 0, :n, lanes] = jnp.where(odd, both_blocks, st_first)
    sum_ref[0, 0, n:, :] = jnp.broadcast_to(dec_ref[2:3, :], (8, dec_ref.shape[1]))


def diag_kernel(odd_ref, xc_ref, xe_ref, s_ref, g_ref, gt_ref, dtt_ref, par_ref, y_ref):
    shift = odd_ref[0]
    odd = shift == 1
    g, gt, dtt = g_ref[0], gt_ref[...], dtt_ref[...]
    t_at = lax.broadcasted_iota(jnp.int32, (HALF, HALF), 0)
    s_at = lax.broadcasted_iota(jnp.int32, (HALF, HALF), 1)
    lower = t_at >= s_at
    left = s_at < 64
    subs = [slice(i * HALF, (i + 1) * HALF) for i in range(3)]
    g_off = jnp.where(odd, g[subs[2]], g[subs[1]])
    behind = [slice(i * HALF, (i + 1) * HALF) for i in range(4)]
    gt_off = jnp.where(odd, gt[:, behind[2]], gt[:, behind[1]])
    dtt_off = jnp.where(odd, dtt[:, behind[2]], dtt[:, behind[1]])
    x_off = xc_ref[pl.ds(pl.multiple_of(shift * HALF, HALF), HALF), :]
    tiles = [
        (g[sub], gt[:, at], dtt[:, at], xc_ref[sub, :]) for sub, at in zip(subs, behind[1:])
    ]
    tiles.append((g_off, gt_off, dtt_off, x_off))
    tiles.append((g[subs[0]], gt[:, behind[0]], dtt[:, behind[0]], xe_ref[...]))
    for pair in range(STEP_HEADS // 2):
        lanes = slice(pair * 128, pair * 128 + 128)
        results = []
        for i, (g_t, g_s, dt_s, x_s) in enumerate(tiles):
            both = []
            for k in range(2):
                h = 2 * pair + k
                gap = g_t[:, h : h + 1] - g_s[h : h + 1]
                if i < 3:
                    gap = jnp.where(lower, gap, -1e30)
                both.append(
                    (s_ref[i] * jnp.exp(gap) * dt_s[h : h + 1]).astype(jnp.bfloat16)
                )
            full = jnp.dot(
                jnp.concatenate(both, 0), x_s[:, lanes], preferred_element_type=jnp.float32
            )
            results.append(jnp.where(left, full[:HALF], full[HALF:]))
        skip = par_ref[5:6, lanes]
        for i in range(3):
            y = results[i] + skip * tiles[i][3][:, lanes].astype(jnp.float32)
            if i == 0:
                y = y + results[4]
            if i == 1:
                y = y + jnp.where(odd, 0.0, results[3])
            if i == 2:
                y = y + jnp.where(odd, results[3], 0.0)
            y_ref[subs[i], lanes] = y


def gate_kernel(
    odd_ref, y_ref, c_ref, ecs_ref, ha_ref, hb_ref, st_ref, dec_ref, z_ref, gain_ref, out_ref, held
):
    early = pl.program_id(0) < 2 - odd_ref[0]
    c = c_ref[...]
    ecs = ecs_ref[...]
    left = lax.broadcasted_iota(jnp.int32, (HALF, 128), 1) < 64
    groups, _, part = ha_ref.shape
    width = 2 * part
    wide = STEP_HEADS * 64
    square = jnp.zeros((HALF, 128), jnp.float32)
    for start in range(0, groups * width, wide):
        group, off = divmod(start, width)
        side, off = divmod(off, part)
        cols = slice(off, off + wide)
        h = (ha_ref, hb_ref)[side][group, :, cols]
        later = h * dec_ref[0:1, start : start + wide] + st_ref[side, group, :, cols]
        hb = jnp.where(early, h, later).astype(jnp.bfloat16)
        far = jnp.dot(c, hb, preferred_element_type=jnp.float32)
        for pair in range(STEP_HEADS // 2):
            head = start // 64 + 2 * pair
            lanes = slice(start + pair * 128, start + pair * 128 + 128)
            scale = jnp.where(left, ecs[:, head : head + 1], ecs[:, head + 1 : head + 2])
            y = y_ref[:, lanes] + far[:, pair * 128 : pair * 128 + 128] * scale
            y = y.astype(jnp.bfloat16).astype(jnp.float32)
            gated = y * silu(z_ref[:, lanes].astype(jnp.float32))
            held[:, lanes] = gated
            square = square + gated * gated
    mean = jnp.sum(square, axis=1, keepdims=True) / (groups * width)
    scale = lax.rsqrt(mean + 1e-5)
    for start in range(0, groups * width, wide):
        lanes = slice(start, start + wide)
        out_ref[:, lanes] = (held[:, lanes] * scale * gain_ref[:, lanes]).astype(jnp.bfloat16)


def params(**more):
    return pltpu.CompilerParams(vmem_limit_bytes=VMEM_BYTES, **more)


def per_device(
    x_in, dt_raw, bc_in, z_in, conv_x, bias_x, conv_bc, bias_bc, dt_bias, a_log, d_skip, norm_gain
):
    f32, bf16 = jnp.float32, jnp.bfloat16
    n_ctx, n_head = lax.axis_size("ctx"), lax.axis_size("head")
    ctx, zed = lax.axis_index("ctx"), lax.axis_index("head")
    rows, width = x_in.shape
    heads = dt_raw.shape[1]
    state = bc_in.shape[1] // 2
    group_width = width // n_head
    group_heads = heads // n_head
    odd = (zed % 2).astype(jnp.int32).reshape(1)

    small = jnp.concatenate([dt_bias, a_log, d_skip])
    small = jnp.pad(small, (0, group_width - small.shape[0]))
    mine = jnp.concatenate([conv_x, bias_x[None], small[None]], 0)
    table = lax.all_gather(mine, "head")
    count = n_ctx * n_head
    rim = jnp.concatenate([x_in[-RIM:], bc_in[-RIM:]], 1)
    rim = lax.ppermute(rim, ("ctx", "head"), [(i, i + 1) for i in range(count - 1)])
    last = rows - HALF - RIM
    to_odd = [(i, i + 1) for i in range(0, n_head, 2)]
    extra_small = lax.ppermute(jnp.concatenate([bc_in[last:], dt_raw[last:]], 1), "head", to_odd)
    deep = rows + HALF
    tail, rim, table, extra_small = lax.optimization_barrier((x_in[last:], rim, table, extra_small))
    extra_x = lax.ppermute(tail, "head", to_odd)
    halo_x, halo_bc = rim[:, :width], rim[:, width:]
    extra_bc, extra_dt = extra_small[:, : 2 * state], extra_small[:, 2 * state :]
    par = jnp.concatenate([table[g] for g in range(n_head)], 1)
    vectors = table[:, 5, : 3 * group_heads].reshape(n_head, 3, group_heads)
    vectors = vectors.transpose(1, 0, 2).reshape(3, heads)
    skip = jnp.repeat(vectors[2], width // heads)
    par = jnp.concatenate([par[:5], skip[None], jnp.zeros((2, width), f32)], 0)

    smem = pl.BlockSpec(memory_space=pltpu.SMEM)
    vmem = pl.BlockSpec(memory_space=pltpu.VMEM)
    shape = jax.ShapeDtypeStruct
    c, bt, scores, g, gt, dtt, wt, ecs, logs = pl.pallas_call(
        prep_kernel,
        in_specs=[smem] + [vmem] * 9,
        out_specs=[vmem] * 9,
        out_shape=[
            shape((rows, state), bf16),
            shape((state, deep), bf16),
            shape((5, HALF, HALF), f32),
            shape((rows, heads), f32),
            shape((heads, deep), f32),
            shape((heads, deep), f32),
            shape((heads, deep), f32),
            shape((rows, heads), f32),
            shape((8, heads), f32),
        ],
        compiler_params=params(),
        name="prep",
    )(
        odd, bc_in, halo_bc, extra_bc, conv_bc, bias_bc[None], dt_raw, extra_dt,
        vectors[0:1], vectors[1:2],
    )
    decays = jnp.repeat(logs, width // heads, axis=1)

    steps = heads // STEP_HEADS
    wide = STEP_HEADS * (width // heads)
    per_group = group_width // wide
    tall = pl.BlockSpec((rows, wide), lambda i: (0, i))
    eight = pl.BlockSpec((8, wide), lambda i: (0, i))
    part = group_width // 2
    per_part = part // wide

    def by_group(depth):
        return pl.BlockSpec(
            (1, 1, depth, wide),
            lambda i: (i // per_part % 2, i // per_group, 0, i % per_part),
        )

    row_heads = pl.BlockSpec((STEP_HEADS, deep), lambda i: (i, 0))

    def whole(*dims):
        return pl.BlockSpec(dims, lambda i: (0,) * len(dims))

    def grouped(depth):
        return shape((2, n_head, depth, part), f32)

    xc, q_first, q_second = pl.pallas_call(
        own_kernel,
        grid=(steps,),
        in_specs=[
            smem,
            tall,
            pl.BlockSpec((RIM, wide), lambda i: (0, i)),
            eight,
            whole(state, deep),
            row_heads,
        ],
        out_specs=[tall, by_group(state), by_group(state)],
        out_shape=[shape((rows, width), bf16), grouped(state), grouped(state)],
        compiler_params=params(),
        cost_estimate=pl.CostEstimate(
            flops=2 * rows * state * width, bytes_accessed=20 * 2**20, transcendentals=rows * width
        ),
        name="own",
    )(odd, x_in, halo_x, par, bt, wt)
    half_tall = pl.BlockSpec((HALF, wide), lambda i: (0, i))
    xe, st_first, summary = pl.pallas_call(
        extra_kernel,
        grid=(steps,),
        in_specs=[
            smem,
            pl.BlockSpec((RIM + HALF, wide), lambda i: (0, i)),
            eight,
            whole(state, deep),
            row_heads,
            eight,
            by_group(state),
            by_group(state),
        ],
        out_specs=[half_tall, by_group(state), by_group(state + 8)],
        out_shape=[shape((HALF, width), bf16), grouped(state), grouped(state + 8)],
        compiler_params=params(),
        cost_estimate=pl.CostEstimate(
            flops=2 * HALF * state * width, bytes_accessed=20 * 2**20, transcendentals=HALF * width
        ),
        name="extra",
    )(odd, extra_x, par, bt, wt, decays, q_first, q_second)

    def exchange(value):
        return lax.all_to_all(value, "head", split_axis=0, concat_axis=0, tiled=True)

    def scan(parts):
        logs = [parts[k, state] for k in range(n_head)]
        total, total_log = parts[0, :state], logs[0]
        for k in range(1, n_head):
            total = total * jnp.exp(logs[k])[None] + parts[k, :state]
            total_log = total_log + logs[k]
        before, before_log = jnp.zeros_like(total), jnp.zeros_like(total_log)
        span = 1
        while span < n_ctx:
            sent = jnp.concatenate([total, jnp.broadcast_to(total_log[None], (8, part))], 0)
            got = lax.ppermute(sent, "ctx", [(i, i ^ span) for i in range(n_ctx)])
            other, other_log = got[:state], got[state]
            upper = ctx // span % 2 == 1
            before = jnp.where(upper, other * jnp.exp(before_log)[None] + before, before)
            before_log = jnp.where(upper, other_log + before_log, before_log)
            total = jnp.where(
                upper,
                other * jnp.exp(total_log)[None] + total,
                total * jnp.exp(other_log)[None] + other,
            )
            total_log = total_log + other_log
            span *= 2
        entries = [before]
        for k in range(n_head - 1):
            entries.append(entries[-1] * jnp.exp(logs[k])[None] + parts[k, :state])
        return jnp.stack(entries)

    parts_a = exchange(summary[0])
    parts_a, later = lax.optimization_barrier((parts_a, summary[1]))
    parts_b = exchange(later)
    entries_a = scan(parts_a)
    entries_a, parts_b = lax.optimization_barrier((entries_a, parts_b))
    h_a = exchange(entries_a)
    entries_b = scan(parts_b)
    entries_b, h_a = lax.optimization_barrier((entries_b, h_a))
    h_b = exchange(entries_b)

    g_steps = g.reshape(rows, steps, STEP_HEADS).transpose(1, 0, 2)
    y_near = pl.pallas_call(
        diag_kernel,
        grid=(steps,),
        in_specs=[
            smem,
            tall,
            half_tall,
            whole(5, HALF, HALF),
            pl.BlockSpec((1, rows, STEP_HEADS), lambda i: (i, 0, 0)),
            row_heads,
            row_heads,
            eight,
        ],
        out_specs=tall,
        out_shape=shape((rows, width), f32),
        compiler_params=params(),
        cost_estimate=pl.CostEstimate(
            flops=10 * 2 * HALF * HALF * width,
            bytes_accessed=20 * 2**20,
            transcendentals=5 * HALF * HALF * heads,
        ),
        name="diag",
    )(odd, xc, xe, scores, g_steps, gt, dtt, par)

    tile = pl.BlockSpec((HALF, width), lambda i: (i, 0))
    narrow = pl.BlockSpec((HALF, heads), lambda i: (i, 0))
    return pl.pallas_call(
        gate_kernel,
        grid=(rows // HALF,),
        in_specs=[
            smem,
            tile,
            pl.BlockSpec((HALF, state), lambda i: (i, 0)),
            narrow,
            whole(n_head, state, part),
            whole(n_head, state, part),
            whole(2, n_head, state, part),
            whole(8, width),
            tile,
            whole(1, width),
        ],
        out_specs=tile,
        out_shape=shape((rows, width), bf16),
        scratch_shapes=[pltpu.VMEM((HALF, width), f32)],
        compiler_params=params(),
        name="gate",
    )(odd, y_near, c, ecs, h_a, h_b, st_first, decays, z_in, norm_gain[None])


def solution(mesh):
    in_specs = (
        P(("ctx", "head"), None),
        P(("ctx", "head"), None),
        P(("ctx", "head"), None),
        P(("ctx", "head"), None),
        P(None, "head"),
        P("head"),
        P(),
        P(),
        P("head"),
        P("head"),
        P("head"),
        P(),
    )
    out_specs = P(("ctx", "head"), None)

    def run(x_in, *rest):
        n_ctx, n_head = mesh.shape["ctx"], mesh.shape["head"]
        rows = x_in.shape[0] // (n_ctx * n_head)
        fits = 2 * rows == 3 * BLOCK and n_head % 2 == 0 and n_ctx & (n_ctx - 1) == 0
        body = per_device if fits else per_device_by_heads
        return jax.shard_map(
            body, mesh=mesh, in_specs=in_specs, out_specs=out_specs, check_vma=False
        )(x_in, *rest)

    return run
```
